256 devices in a mesh: mpo: 4 (over y), sector: 64 (over z, x, core).
Axes of the slice: x: 4, y: 4, z: 8, core: 2. Of those that a mesh axis runs over, the one named last changes fastest.
Arguments:
- wavefunction: bfloat16 [8192, 64, 128], P('sector'), may hold values from -6 to 6
- left_env: bfloat16 [8, 8192, 128], P('mpo', 'sector'), may hold values from -4 to 4
- right_env: bfloat16 [8, 8192, 128], P('mpo', 'sector'), may hold values from -2 to 2
- term_live: int32 [8, 64], P('mpo', 'sector'), may hold values 0 or 1
- block_live: int32 [64, 64], P('sector'), may hold values from 0 to 1, as said below
- sector_dims: int32 [64], replicated, may hold values from 96 to 128, as said below
Outputs:
- residual: bfloat16 [8192, 64, 128], P('sector')
- second_image: bfloat16 [8192, 64, 128], P('sector')
The draws below stay inside these ranges and needn't reach their ends.
Inputs may be any that keep to these rules, and one draw needn't show every extreme that they name: `block_live`: every diagonal block (a, a) is allowed. `sector_dims`: some sector has all 128 rows used.
All inputs are finite; a program needn't handle non-finite values. No bound on the sum of `term_live` on one device may be relied on, other than what follows from the above.
Results may differ from the reference program's by a relative error of at most 0.025.
Values may be sent and summed in bfloat16 or wider, within the bound.
A program may use at most 64 MiB of HBM per device.

```python
import jax
import jax.numpy as jnp
from jax import lax

BLOCK = 128
TERMS_DEV = 2
TERMS = 8
SECTORS = 64
N_MPO = 4


def draw_block_live(key, part):
    key = jax.random.fold_in(key, 11)
    coins = (jax.random.randint(key, (SECTORS, SECTORS), 0, 4) < 3).astype(jnp.int32)
    diagonal = lax.broadcasted_iota(jnp.int32, (SECTORS, SECTORS), 0) == lax.broadcasted_iota(jnp.int32, (SECTORS, SECTORS), 1)
    return jnp.where(diagonal, 1, coins).astype(jnp.int32)


def draw_sector_dims(key, part):
    key = jax.random.fold_in(key, 23)
    first_key, second_key = jax.random.split(key)
    values = jax.random.randint(first_key, (SECTORS,), 3 * BLOCK // 4, BLOCK + 1)
    chosen = jax.random.randint(second_key, (), 0, SECTORS)
    sectors = jnp.arange(SECTORS, dtype=jnp.int32)
    return jnp.where(sectors == chosen, BLOCK, values).astype(jnp.int32)


def env_pieces(key, noise_scale):
    shape = (TERMS, SECTORS * BLOCK, BLOCK)
    rows = lax.broadcasted_iota(jnp.int32, shape, 1)
    cols = lax.broadcasted_iota(jnp.int32, shape, 2)
    diagonal = (rows % BLOCK == cols).astype(jnp.float32)
    sector_pos = (rows // BLOCK).astype(jnp.float32) / float(max(SECTORS - 1, 1))
    noise = jnp.clip(jax.random.normal(key, shape, jnp.float32), -4.0, 4.0)
    return (diagonal + noise * (noise_scale / jnp.sqrt(jnp.float32(BLOCK))), sector_pos)


def draw_left_env(key, part):
    key = jax.random.fold_in(key, 37)
    block, sector_pos = env_pieces(key, 0.5)
    rise = 1.0 + 4.0 * sector_pos
    return (block * rise / float(TERMS)).astype(jnp.bfloat16)


def draw_right_env(key, part):
    key = jax.random.fold_in(key, 41)
    block, sector_pos = env_pieces(key, 0.5)
    return block.astype(jnp.bfloat16)


def place_ends(entries, rng, smallest, largest):
    dims = entries.shape
    place = [jax.random.randint(jax.random.fold_in(rng, axis), (), 0, dims[axis]) for axis in range(len(dims))]
    entries = entries.at[tuple(place)].set(smallest)
    longest = dims.index(max(dims))
    place[longest] = (place[longest] + 1) % dims[longest]
    return entries.at[tuple(place)].set(largest)


def steps_of(rng, extent, cuts, low, top_value):
    def one(axis_at, shards_of):
        steps = jax.random.uniform(jax.random.fold_in(jax.random.fold_in(rng, 6), axis_at), (shards_of,), jnp.float32, low / len(cuts), top_value / len(cuts))
        return jnp.repeat(jnp.exp(steps), extent[axis_at] // shards_of).reshape((-1,) + (1,) * (len(extent) - axis_at - 1))

    gain = one(*cuts[0])
    for cut in cuts[1:]:
        gain = gain * one(*cut)
    return gain


def gaussian(own_key, shape, spread, reach, pieces=(), kind=jnp.bfloat16):
    drawn = jax.random.normal(own_key, shape, jnp.float32) * spread
    if len(pieces) > 0:
        drawn = steps_of(own_key, shape, pieces, -0.22, 0.18) * drawn
    return jnp.clip(drawn, min=-reach, max=reach).astype(kind)


def setup_inputs(seed: int = 0) -> dict:
    key_list = jax.random.split(jax.random.key(seed), 7)
    wavefunction = gaussian(key_list[0], (SECTORS * BLOCK, SECTORS, BLOCK), 1.0, 6.0, ((0, 64),))
    left_env = draw_left_env(jax.random.fold_in(key_list[6], 71), 0)
    right_env = draw_right_env(jax.random.fold_in(key_list[6], 71), 0)
    term_live = place_ends((jax.random.randint(key_list[3], (TERMS, SECTORS), 0, 3) < 2).astype(jnp.int32), jax.random.fold_in(key_list[3], 1), 0, 1)
    block_live = draw_block_live(jax.random.fold_in(key_list[6], 71), 0)
    sector_dims = draw_sector_dims(jax.random.fold_in(key_list[6], 71), 0)
    return dict(wavefunction=wavefunction, left_env=left_env, right_env=right_env, term_live=term_live, block_live=block_live, sector_dims=sector_dims)


def reference(wavefunction, left_env, right_env, term_live, block_live, sector_dims):
    positions = jnp.arange(BLOCK, dtype=jnp.int32)
    inside = positions[None, :] < sector_dims[:, None]
    live = (block_live[:, None, :, None] > 0) & inside[:, :, None, None] & inside[None, None, :, :]
    blocks = wavefunction.reshape(SECTORS, BLOCK, SECTORS, BLOCK)
    state = jnp.where(live, blocks, jnp.zeros_like(blocks))
    lefts = left_env.reshape(TERMS, SECTORS, BLOCK, BLOCK) * term_live.astype(jnp.bfloat16)[:, :, None, None]
    lefts = lefts.reshape(N_MPO, TERMS_DEV, SECTORS, BLOCK, BLOCK)
    rights = right_env.reshape(N_MPO, TERMS_DEV, SECTORS, BLOCK, BLOCK)

    def apply_h(vector):
        wide = vector.astype(jnp.float32)

        def one_term(total, pair):
            left_block, right_block = pair
            half = jnp.einsum('aik,akbj->aibj', left_block.astype(jnp.float32), wide).astype(jnp.bfloat16)
            more = jnp.einsum('aibk,bkj->aibj', half.astype(jnp.float32), right_block.astype(jnp.float32))
            return total + more, None

        def one_group(total, pair):
            group_sum, _ = lax.scan(one_term, jnp.zeros(wide.shape, jnp.float32), pair)
            rounded = lax.optimization_barrier(group_sum.astype(jnp.bfloat16))
            return total + rounded.astype(jnp.float32), None

        summed, _ = lax.scan(one_group, jnp.zeros(wide.shape, jnp.float32), (lefts, rights))
        return jnp.where(live, summed, jnp.zeros_like(summed)).astype(jnp.bfloat16)

    first = apply_h(state)
    state_wide = state.astype(jnp.float32)
    first_wide = first.astype(jnp.float32)
    rayleigh = jnp.sum(state_wide * first_wide) / jnp.sum(state_wide * state_wide)
    residual = (first_wide - rayleigh * state_wide).astype(jnp.bfloat16)
    second_image = apply_h(residual)
    shape_out = (SECTORS * BLOCK, SECTORS, BLOCK)
    return residual.reshape(shape_out), second_image.reshape(shape_out)
```

```python
import jax
import jax.numpy as jnp
from jax import lax
from jax.sharding import PartitionSpec as P

Z, X, C = 8, 4, 2


def body(wavefunction, left_env, right_env, term_live, block_live, sector_dims):
    n = wavefunction.shape[0]
    y_at = lax.axis_index("mpo")
    s_at = lax.axis_index("sector")
    places = jnp.arange(n, dtype=jnp.int32)
    inside = places[None, :] < sector_dims[:, None]
    own_rows = lax.dynamic_index_in_dim(inside, s_at, 0, keepdims=False)
    mask = (block_live[0] > 0)[None, :, None] & own_rows[:, None, None] & inside[None]
    state = jnp.where(mask, wavefunction, jnp.zeros_like(wavefunction))

    order = []
    for y in range(X):
        for z in range(Z):
            for x in range(X):
                for c in range(C):
                    order.append((y * Z * X * C + (z * X + x) * C + c, x * Z * X * C + (z * X + y) * C + c))
    right_here = lax.ppermute(right_env, ("mpo", "sector"), order)
    rights = lax.all_gather(right_here, "sector").reshape(Z, X, C, 2, n, n)
    rights = rights.transpose(0, 2, 1, 3, 4, 5).reshape(Z * C, 2 * X, n, n)
    lefts = jnp.where((term_live > 0)[:, :, None], left_env, jnp.zeros_like(left_env))
    lefts = lax.all_gather(lefts, "mpo", tiled=True)

    def own(full):
        part = lax.dynamic_index_in_dim(full.reshape(n, Z, X, C, n), y_at, 2, keepdims=False)
        return part.reshape(n, Z * C, n)

    mask_own = own(mask)

    def apply_own(vector):
        half = jnp.einsum("tik,kbj->btij", lefts, vector, preferred_element_type=jnp.float32).astype(jnp.bfloat16)
        image = jnp.einsum("btik,btkj->bij", half, rights, preferred_element_type=jnp.float32)
        image = image.transpose(1, 0, 2)
        return jnp.where(mask_own, image, 0.0).astype(jnp.bfloat16)

    def share(part):
        full = lax.all_gather(part, "mpo").reshape(X, n, Z, C, n)
        return full.transpose(1, 2, 0, 3, 4).reshape(n, Z * X * C, n)

    state_own = own(state)
    first_own = apply_own(state_own)
    wide, first_wide = state_own.astype(jnp.float32), first_own.astype(jnp.float32)
    sums = lax.psum(jnp.stack([jnp.sum(wide * first_wide), jnp.sum(wide * wide)]), ("mpo", "sector"))
    residual_own = (first_wide - sums[0] / sums[1] * wide).astype(jnp.bfloat16)
    second_own = apply_own(residual_own)
    return share(residual_own), share(second_own)


def solution(mesh):
    return jax.shard_map(
        body,
        mesh=mesh,
        in_specs=(
            P("sector", None, None),
            P("mpo", "sector", None),
            P("mpo", "sector", None),
            P("mpo", "sector"),
            P("sector", None),
            P(),
        ),
        out_specs=(P("sector", None, None), P("sector", None, None)),
        check_vma=False,
    )
```

```python
import jax
import jax.numpy as jnp
from jax import lax
from jax.experimental import pallas as pl
from jax.experimental.pallas import tpu as pltpu
from jax.sharding import PartitionSpec as P

MESH = pl.DeviceIdType.MESH
Y, Z, X, C = 4, 8, 4, 2
N = 128
T = 8


def wrap(value, size):
    return lax.rem(value + size, size)


def images_kernel(
    v_ref, l_ref, r_ref, rows_ref, cols_ref,
    fg_ref, tot_ref,
    lcat, rbuf, xbuf, own, sums, sent, got,
    l_send, l_recv, r_send, r_recv, z_send, z_recv, c_send, c_recv,
    y_send, y_recv, f_send, o_sem, a_send, a_recv,
):
    y, s = lax.axis_index("mpo"), lax.axis_index("sector")
    z, x, c = s // (X * C), lax.rem(s // C, X), lax.rem(s, C)

    def place(y_at, z_at, x_at, c_at):
        return (y_at, (z_at * X + x_at) * C + c_at)

    def remote(src, dst, send, recv, device):
        return pltpu.make_async_remote_copy(
            src_ref=src, dst_ref=dst, send_sem=send, recv_sem=recv, device_id=device, device_id_type=MESH
        )

    here = place(y, z, x, c)
    y_near = [place(wrap(y + k, Y), z, x, c) for k in range(Y)]
    z_near = [place(y, wrap(z + k, Z), x, c) for k in range(Z)]
    x_near = [place(y, z, wrap(x + k, X), c) for k in range(X)]
    sibling = place(y, z, x, 1 - c)

    barrier = pltpu.get_barrier_semaphore()
    sources = y_near[1:] + z_near[1:] + x_near[1:] + [sibling] + [place(p, z, y, c) for p in range(Y)]
    for device in sources:
        pl.semaphore_signal(barrier, inc=1, device_id=device, device_id_type=MESH)
    pl.semaphore_wait(barrier, len(sources))

    l_copies = []
    for k in range(1, Y):
        copy = remote(l_ref, lcat.at[pl.ds(2 * y, 2)], l_send.at[k - 1], l_recv.at[k - 1], y_near[k])
        copy.start()
        l_copies.append(copy)

    def row_copy(k):
        return remote(
            r_ref, rbuf.at[z, c, pl.ds(2 * y, 2)], r_send.at[k], r_recv.at[y], place(x, z, wrap(x + k, X), c)
        )

    for k in range(1, X):
        row_copy(k).start()

    @pl.when(x == y)
    def _():
        pltpu.make_async_copy(r_ref, rbuf.at[z, c, pl.ds(2 * y, 2)], r_recv.at[y]).start()

    @pl.when(x != y)
    def _():
        row_copy(0).start()

    lcat[pl.ds(2 * y, 2)] = l_ref[...]
    for k in range(1, Y):
        from_y = wrap(y - k, Y)
        remote(l_ref, lcat.at[pl.ds(2 * from_y, 2)], l_send.at[k - 1], l_recv.at[k - 1], here).wait_recv()

    def masked(z_at, c_at):
        mask = rows_ref[...] * cols_ref[(z_at * Y + y) * C + c_at]
        return mask, v_ref[z_at, c_at].astype(jnp.float32) * mask

    def contract_left(vector):
        left = lcat[...].reshape(T * N, N)
        half = jnp.dot(left, vector, preferred_element_type=jnp.float32).astype(jnp.bfloat16)
        return half.reshape(T, N, half.shape[1])

    def beside(half):
        return jnp.concatenate([half[t] for t in range(T)], axis=1)

    def first_halves(z_at, carry):
        pair = [masked(z_at, c_at)[1].astype(jnp.bfloat16) for c_at in range(C)]
        half = contract_left(jnp.concatenate(pair, axis=1))
        for c_at in range(C):
            xbuf[z_at, c_at] = beside(half[:, :, c_at * N : (c_at + 1) * N])
        return carry

    lax.fori_loop(0, Z, first_halves, 0)
    sums[...] = jnp.zeros_like(sums)

    def images(z_at):
        def one(c_at, carry):
            mask, state = masked(z_at, c_at)
            right = rbuf[z_at, c_at].reshape(T * N, N)
            image = jnp.dot(xbuf[z_at, c_at], right, preferred_element_type=jnp.float32) * mask
            first = image.astype(jnp.bfloat16)
            own[z_at, c_at, 0] = first
            sums[0] += state * first.astype(jnp.float32)
            sums[1] += state * state
            half = beside(contract_left(first))
            image = jnp.dot(half, right, preferred_element_type=jnp.float32) * mask
            own[z_at, c_at, 1] = image.astype(jnp.bfloat16)
            return carry

        lax.fori_loop(0, C, one, 0)

    order = [z]
    for d in range(1, Z // 2):
        order += [wrap(z - d, Z), wrap(z + d, Z)]
    order.append(wrap(z + Z // 2, Z))

    def ring_copy(m, device):
        block = rbuf.at[order[m], c]
        return remote(block, block, z_send.at[m], z_recv.at[m], device)

    def hand_over(m, c_at):
        block = rbuf.at[order[m], c_at]
        return remote(block, block, c_send.at[m], c_recv.at[m], sibling)

    def send_images(m, sign):
        return remote(
            own.at[order[m]], fg_ref.at[order[m], y], y_send.at[m, sign], y_recv.at[m, sign], y_near[1 if sign == 0 else 3]
        )

    def keep_images(m):
        return pltpu.make_async_copy(own.at[order[m]], fg_ref.at[order[m], y], o_sem.at[m])

    def arrived(m, sign):
        from_y = wrap(y + (3, 1, 2)[sign], Y)
        block = fg_ref.at[order[m], from_y]
        return remote(block, block, y_send.at[m, 0], y_recv.at[m, sign], here)

    def forward(m):
        sign = m % 2
        arrived(m, sign).wait_recv()
        from_y = wrap(y + (3, 1)[sign], Y)
        block = fg_ref.at[order[m], from_y]
        remote(block, block, f_send.at[m], y_recv.at[m, 2], y_near[1 if sign == 0 else 3]).start()

    def onward(m):
        if m == 0:
            return [(0, 1, z_near[1]), (0, 2, z_near[Z - 1])]
        if m < Z - 3:
            return [(m, m + 2, z_near[1 if m % 2 else Z - 1])]
        return []

    def pass_on(m):
        for src, dst, device in onward(m):
            block = rbuf.at[order[src], c]
            remote(block, block, z_send.at[dst], z_recv.at[dst], device).start()

    def pass_last():
        source = lax.select(c == 0, wrap(z - 3, Z), wrap(z + 3, Z))
        target = place(y, lax.select(c == 0, wrap(z + 1, Z), wrap(z - 1, Z)), x, c)
        block = rbuf.at[source, c]
        return remote(block, block, z_send.at[Z - 1], z_recv.at[Z - 1], target)

    for m in range(Z):
        if m == 0:
            for p in range(Y):
                part = rbuf.at[z, c, pl.ds(2 * p, 2)]
                remote(part, part, r_send.at[0], r_recv.at[p], here).wait_recv()
        else:
            ring_copy(m, here).wait_recv()
        hand_over(m, c).start()
        pass_on(m)
        if m == Z - 2:
            pass_last().start()
        hand_over(m, 1 - c).wait_recv()
        images(order[m])
        send_images(m, 0).start()
        send_images(m, 1).start()
        keep_images(m).start()
        if m >= 2:
            forward(m - 2)

    row = lax.broadcasted_iota(jnp.int32, (8, N), 0)
    part = [jnp.sum(sums[k], axis=0, keepdims=True) for k in range(2)]
    sent[0] = jnp.where(row == 0, part[0], 0.0) + jnp.where(row == 1, part[1], 0.0)
    rounds = [(x, x_near[1:]), (z, z_near[1:]), (c, [sibling]), (y, y_near[1:])]
    base = 0
    for step, (at, devices) in enumerate(rounds):
        copies = []
        for k, device in enumerate(devices):
            copy = remote(sent.at[step], got.at[base + at], a_send.at[base + k], a_recv.at[base + k], device)
            copy.start()
            copies.append(copy)
        got[base + at] = sent[step]
        if step == 1:
            forward(Z - 2)
        if step == 3:
            forward(Z - 1)
        for copy in copies:
            copy.wait()
        total = got[base]
        for k in range(len(devices)):
            total += got[base + 1 + k]
        if step + 1 < len(rounds):
            sent[step + 1] = total
        else:
            tot_ref[...] = total
        base += len(devices) + 1

    for m in range(Z):
        arrived(m, 1 - m % 2).wait_recv()
        arrived(m, 2).wait_recv()
        keep_images(m).wait()
        send_images(m, 0).wait_send()
        send_images(m, 1).wait_send()
        remote(fg_ref.at[0, 0], fg_ref.at[0, 0], f_send.at[m], y_recv.at[m, 2], here).wait_send()
        hand_over(m, c).wait_send()
        if m > 0:
            ring_copy(m, here).wait_send()
    for copy in l_copies:
        copy.wait_send()
    for k in range(1, X):
        row_copy(k).wait_send()

    @pl.when(x != y)
    def _():
        row_copy(0).wait_send()


def images_call(v, left, right, rows, cols):
    vmem = pl.BlockSpec(memory_space=pltpu.VMEM)
    dma = pltpu.SemaphoreType.DMA
    bf16, f32 = jnp.bfloat16, jnp.float32
    rounds = X + Z + C + Y
    return pl.pallas_call(
        images_kernel,
        out_shape=(
            jax.ShapeDtypeStruct((Z, Y, C, 2, N, N), bf16),
            jax.ShapeDtypeStruct((8, N), f32),
        ),
        in_specs=[vmem] * 5,
        out_specs=(pl.BlockSpec(memory_space=pl.ANY), vmem),
        scratch_shapes=[
            pltpu.VMEM((T, N, N), bf16),
            pltpu.VMEM((Z, C, T, N, N), bf16),
            pltpu.VMEM((Z, C, N, T * N), bf16),
            pltpu.VMEM((Z, C, 2, N, N), bf16),
            pltpu.VMEM((2, N, N), f32),
            pltpu.VMEM((4, 8, N), f32),
            pltpu.VMEM((rounds, 8, N), f32),
            dma((Y - 1,)), dma((Y - 1,)),
            dma((X,)), dma((Y,)),
            dma((Z,)), dma((Z,)),
            dma((Z,)), dma((Z,)),
            dma((Z, 2)), dma((Z, 3)),
            dma((Z,)), dma((Z,)),
            dma((rounds,)), dma((rounds,)),
        ],
        compiler_params=pltpu.CompilerParams(collective_id=0, has_side_effects=True, vmem_limit_bytes=40 << 20),
    )(v, left, right, rows, cols)


def finish_kernel(tot_ref, w_ref, rows_ref, cols_ref, fg_ref, residual_ref, second_ref):
    tot = tot_ref[...]
    over = jnp.sum(tot[0:1], axis=1, keepdims=True)
    under = jnp.sum(tot[1:2], axis=1, keepdims=True)
    rayleigh = (over / under)[None]
    first = jnp.swapaxes(fg_ref[:, 0].astype(jnp.float32), 0, 1)
    image = jnp.swapaxes(fg_ref[:, 1].astype(jnp.float32), 0, 1)
    state = w_ref[...].astype(jnp.float32) * rows_ref[...] * cols_ref[...][None]
    residual_ref[...] = (first - rayleigh * state).astype(jnp.bfloat16)
    second_ref[...] = (image - rayleigh * first).astype(jnp.bfloat16)


def finish_call(tot, w, rows, cols, fg):
    step = 16
    sectors = w.shape[1]
    shape = jax.ShapeDtypeStruct(w.shape, w.dtype)
    slab = pl.BlockSpec((step, sectors, N), lambda i: (i, 0, 0))
    return pl.pallas_call(
        finish_kernel,
        grid=(N // step,),
        out_shape=(shape, shape),
        in_specs=[
            pl.BlockSpec((8, N), lambda i: (0, 0)),
            slab,
            pl.BlockSpec((step, 1, N), lambda i: (i, 0, 0)),
            pl.BlockSpec((sectors, N), lambda i: (0, 0)),
            pl.BlockSpec((sectors, 2, step, N), lambda i: (0, 0, i, 0)),
        ],
        out_specs=(slab, slab),
        compiler_params=pltpu.CompilerParams(vmem_limit_bytes=40 << 20),
    )(tot, w, rows, cols, fg)


def body(wavefunction, left_env, right_env, term_live, block_live, sector_dims):
    y, s = lax.axis_index("mpo"), lax.axis_index("sector")
    sectors = wavefunction.shape[1]
    places = jnp.arange(N, dtype=jnp.int32)
    own_dim = lax.dynamic_index_in_dim(sector_dims, s, 0, keepdims=False)
    rows = jnp.broadcast_to((places < own_dim).astype(jnp.float32)[:, None], (N, N))
    cols = ((block_live[0] > 0)[:, None] & (places[None, :] < sector_dims[:, None])).astype(jnp.float32)
    left = jnp.where((term_live > 0)[:, :, None], left_env, jnp.zeros_like(left_env))
    v = lax.dynamic_index_in_dim(wavefunction.reshape(N, Z, X, C, N), y, 2, keepdims=False)
    v = v.transpose(1, 2, 0, 3)
    fg, tot = images_call(v, left, right_env, rows, cols.reshape(sectors, 1, N))
    return finish_call(tot, wavefunction, rows.reshape(N, 1, N), cols, fg.reshape(sectors, 2, N, N))


def solution(mesh):
    return jax.shard_map(
        body,
        mesh=mesh,
        in_specs=(
            P("sector", None, None),
            P("mpo", "sector", None),
            P("mpo", "sector", None),
            P("mpo", "sector"),
            P("sector", None),
            P(),
        ),
        out_specs=(P("sector", None, None), P("sector", None, None)),
        check_vma=False,
    )
```

```python
import jax
import jax.numpy as jnp
from jax import lax
from jax.experimental import pallas as pl
from jax.experimental.pallas import tpu as pltpu
from jax.sharding import PartitionSpec as P

MESH = pl.DeviceIdType.MESH
Y, Z, X, C = 4, 8, 4, 2
B = Z * X * C
N = 128
PAIR = 2
T = Y * PAIR
PIECES = 2


def wrap(value, size):
    return lax.rem(value + size, size)


def images_kernel(
    live_hbm, block_hbm, dims_hbm, w_ref, l_ref, r_ref,
    fg_ref, tot_ref, rows_ref, cols_ref,
    live_ref, block_ref, dims_ref, wide, wbuf, lown, lcat, rbuf, xbuf, own, sums, sent, got,
    in_sem, l_send, l_recv, r_send, r_recv, z_send, z_recv, c_send, c_recv,
    y_send, y_recv, f_send, o_sem, a_send, a_recv,
):
    y, s = lax.axis_index("mpo"), lax.axis_index("sector")
    z, x, c = s // (X * C), lax.rem(s // C, X), lax.rem(s, C)

    def place(y_at, z_at, x_at, c_at):
        return (y_at, (z_at * X + x_at) * C + c_at)

    def remote(src, dst, send, recv, device):
        return pltpu.make_async_remote_copy(
            src_ref=src, dst_ref=dst, send_sem=send, recv_sem=recv, device_id=device, device_id_type=MESH
        )

    here = place(y, z, x, c)
    z_near = [place(y, wrap(z + k, Z), x, c) for k in range(Z)]
    y_near = [place(wrap(y + k, Y), z, x, c) for k in range(Y)]
    sibling = place(y, z, x, 1 - c)
    plane = [place(wrap(y + i, Y), z, wrap(x + j, X), c) for i in range(Y) for j in range(X)][1:]
    line = [place(y, wrap(z + i, Z), x, wrap(c + j, C)) for i in range(Z) for j in range(C)][1:]

    barrier = pltpu.get_barrier_semaphore()
    for device in plane + line:
        pl.semaphore_signal(barrier, inc=1, device_id=device, device_id_type=MESH)
    sources = (live_hbm, l_ref, block_hbm, dims_hbm, w_ref)
    targets = (live_ref, lown, block_ref, dims_ref, wbuf)
    fetch = [pltpu.make_async_copy(src, dst, in_sem.at[k]) for k, (src, dst) in enumerate(zip(sources, targets))]
    for copy in fetch:
        copy.start()
    fetch[0].wait()
    fetch[1].wait()
    for k in range(PAIR):
        lown[k] = jnp.where(live_ref[0, k] > 0, lown[k].astype(jnp.float32), 0.0).astype(jnp.bfloat16)
    lcat[pl.ds(2 * y, PAIR)] = lown[...]
    pl.semaphore_wait(barrier, len(plane) + len(line))

    def row_copy(k):
        return remote(
            r_ref, rbuf.at[z, c, pl.ds(2 * y, PAIR)], r_send.at[k], r_recv.at[y], place(x, z, wrap(x + k, X), c)
        )

    for k in range(1, X):
        row_copy(k).start()

    @pl.when(x == y)
    def _():
        pltpu.make_async_copy(r_ref, rbuf.at[z, c, pl.ds(2 * y, PAIR)], r_recv.at[y]).start()

    @pl.when(x != y)
    def _():
        row_copy(0).start()

    def left_copy(k, device):
        from_y = wrap(y - k, Y) if device is here else y
        return remote(lown, lcat.at[pl.ds(2 * from_y, PAIR)], l_send.at[k - 1], l_recv.at[k - 1], device)

    for k in range(1, Y):
        left_copy(k, y_near[k]).start()

    for copy in fetch[2:]:
        copy.wait()

    def widen(i, carry):
        chunk = wbuf[pl.ds(i * 16, 16)].astype(jnp.float32)
        wide[pl.ds(i * 16 * B, 16 * B), :] = chunk.reshape(16 * B, N)
        return carry

    lax.fori_loop(0, N // 16, widen, 0)

    rows = lax.broadcasted_iota(jnp.int32, (N, N), 0)
    lanes = lax.broadcasted_iota(jnp.int32, (N, N), 1)
    own_dim = dims_ref[s]

    def used(b):
        return jnp.where(block_ref[0, b] > 0, dims_ref[b], 0)

    def masked(z_at, c_at):
        b = (z_at * X + y) * C + c_at
        mask = (rows < own_dim) & (lanes < used(b))
        return mask, jnp.where(mask, wide[pl.ds(b, N, stride=B), :], 0.0)

    def contract_left(vector):
        left = lcat[...].reshape(T * N, N)
        half = jnp.dot(left, vector, preferred_element_type=jnp.float32).astype(jnp.bfloat16)
        return half.reshape(T, N, half.shape[1])

    def beside(half):
        return jnp.concatenate([half[t] for t in range(T)], axis=1)

    def first_halves(z_at, carry):
        pair = [masked(z_at, c_at)[1].astype(jnp.bfloat16) for c_at in range(C)]
        half = contract_left(jnp.concatenate(pair, axis=1))
        for c_at in range(C):
            xbuf[z_at, c_at] = beside(half[:, :, c_at * N : (c_at + 1) * N])
        return carry

    sums[...] = jnp.zeros_like(sums)

    def images(z_at):
        def one(c_at, carry):
            mask, state = masked(z_at, c_at)
            right = rbuf[z_at, c_at].reshape(T * N, N)
            image = jnp.dot(xbuf[z_at, c_at], right, preferred_element_type=jnp.float32)
            first = jnp.where(mask, image, 0.0).astype(jnp.bfloat16)
            own[z_at, c_at, 0] = first
            sums[0] += state * first.astype(jnp.float32)
            sums[1] += state * state
            image = jnp.dot(beside(contract_left(first)), right, preferred_element_type=jnp.float32)
            own[z_at, c_at, 1] = jnp.where(mask, image, 0.0).astype(jnp.bfloat16)
            return carry

        lax.fori_loop(0, C, one, 0)

    order = [z]
    for d in range(1, Z // 2):
        order += [wrap(z - d, Z), wrap(z + d, Z)]
    order.append(wrap(z + Z // 2, Z))
    terms = T // PIECES

    def ring_copy(z_at, m, k, device):
        block = rbuf.at[z_at, c, pl.ds(k * terms, terms)]
        return remote(block, block, z_send.at[m, k], z_recv.at[m, k], device)

    def hand_over(m, k, c_at):
        block = rbuf.at[order[m], c_at, pl.ds(k * terms, terms)]
        return remote(block, block, c_send.at[m, k], c_recv.at[m, k], sibling)

    def onward(m):
        if m == 0:
            return [(order[0], 1, z_near[1]), (order[0], 2, z_near[Z - 1])]
        if m < Z - 3:
            return [(order[m], m + 2, z_near[1 if m % 2 else Z - 1])]
        if m == Z - 2:
            source = lax.select(c == 0, order[Z - 3], order[Z - 2])
            return [(source, Z - 1, place(y, lax.select(c == 0, wrap(z + 1, Z), wrap(z - 1, Z)), x, c))]
        return []

    def ring(m, k):
        if m == 0:
            for p in range(k * terms // PAIR, (k + 1) * terms // PAIR):
                part = rbuf.at[z, c, pl.ds(PAIR * p, PAIR)]
                remote(part, part, r_send.at[0], r_recv.at[p], here).wait_recv()
        else:
            ring_copy(order[m], m, k, here).wait_recv()
        for z_at, to, device in onward(m):
            ring_copy(z_at, to, k, device).start()
        hand_over(m, k, c).start()

    def keep_images(m):
        return pltpu.make_async_copy(own.at[order[m]], fg_ref.at[order[m], y], o_sem.at[m])

    def send_images(m, way):
        return remote(
            own.at[order[m]], fg_ref.at[order[m], y], y_send.at[m, way], y_recv.at[m, way], y_near[(1, Y - 1)[way]]
        )

    def arrived(m, way):
        block = fg_ref.at[order[m], wrap(y + (3, 1, 2)[way], Y)]
        return remote(block, block, y_send.at[m, 0], y_recv.at[m, way], here)

    def forward(m, device=None):
        way = m % 2
        block = fg_ref.at[order[m], wrap(y + (3, 1)[way], Y)]
        return remote(block, block, f_send.at[m], y_recv.at[m, 2], y_near[(1, Y - 1)[way]])

    def pass_images(m):
        arrived(m, m % 2).wait_recv()
        forward(m).start()

    def compute(m):
        for k in range(PIECES):
            hand_over(m, k, 1 - c).wait_recv()
        images(order[m])
        send_images(m, 0).start()
        send_images(m, 1).start()
        keep_images(m).start()

    def sum_copy(step, k):
        at = (y * X + x, z * C + c)[step]
        return remote(
            sent.at[step], got.at[step, at], a_send.at[step, k], a_recv.at[step, k], (plane, line)[step][k]
        )

    def start_sum(step):
        for k in range(15):
            sum_copy(step, k).start()
        got[step, (y * X + x, z * C + c)[step]] = sent[step]

    def end_sum(step):
        for k in range(15):
            sum_copy(step, k).wait()
        total = got[step, 0]
        for k in range(1, 16):
            total += got[step, k]
        return total

    ring(0, 0)
    for k in range(1, Y):
        left_copy(k, here).wait_recv()
    lax.fori_loop(0, Z, first_halves, 0)
    ring(0, 1)
    compute(0)
    for d in range(1, Z // 2):
        near = (2 * d - 1, 2 * d)
        for m in near:
            ring(m, 0)
        if d == 3:
            pass_images(2)
        for m in near:
            ring(m, 1)
        for m in near:
            compute(m)
        pass_images((0, 1, 3)[d - 1])
    for k in range(PIECES):
        ring(Z - 1, k)
    compute(Z - 1)

    row = lax.broadcasted_iota(jnp.int32, (8, N), 0)
    part = [jnp.sum(sums[k], axis=0, keepdims=True) for k in range(2)]
    sent[0] = jnp.where(row == 0, part[0], 0.0) + jnp.where(row == 1, part[1], 0.0)
    start_sum(0)

    def columns(b, carry):
        cols_ref[pl.ds(b, 1), :] = jnp.where(lanes[:1] < used(b), 1.0, 0.0)
        return carry

    lax.fori_loop(0, B, columns, 0)
    rows_ref[...] = jnp.where(rows < own_dim, 1.0, 0.0)
    for m in range(Z - 4, Z - 2):
        pass_images(m)
    sent[1] = end_sum(0)
    start_sum(1)
    for m in range(Z - 2, Z):
        pass_images(m)
    tot_ref[...] = end_sum(1)

    for m in range(Z):
        arrived(m, 1 - m % 2).wait_recv()
        arrived(m, 2).wait_recv()
        keep_images(m).wait()
        send_images(m, 0).wait_send()
        send_images(m, 1).wait_send()
        forward(m).wait_send()
        for k in range(PIECES):
            hand_over(m, k, c).wait_send()
            if m > 0:
                ring_copy(order[m], m, k, here).wait_send()
    for k in range(1, Y):
        left_copy(k, here).wait_send()
    for k in range(1, X):
        row_copy(k).wait_send()

    @pl.when(x != y)
    def _():
        row_copy(0).wait_send()


def images_call(live, block, dims, w, left, right):
    vmem = pl.BlockSpec(memory_space=pltpu.VMEM)
    dma = pltpu.SemaphoreType.DMA
    bf16, f32 = jnp.bfloat16, jnp.float32
    return pl.pallas_call(
        images_kernel,
        out_shape=(
            jax.ShapeDtypeStruct((Z, Y, C, 2, N, N), bf16),
            jax.ShapeDtypeStruct((8, N), f32),
            jax.ShapeDtypeStruct((N, N), f32),
            jax.ShapeDtypeStruct((B, N), f32),
        ),
        in_specs=[pl.BlockSpec(memory_space=pltpu.HBM)] * 6,
        out_specs=(pl.BlockSpec(memory_space=pl.ANY),) + (vmem,) * 3,
        scratch_shapes=[
            pltpu.SMEM((1, PAIR), jnp.int32),
            pltpu.SMEM((1, B), jnp.int32),
            pltpu.SMEM((B,), jnp.int32),
            pltpu.VMEM((N * B, N), f32),
            pltpu.VMEM((N, B, N), bf16),
            pltpu.VMEM((PAIR, N, N), bf16),
            pltpu.VMEM((T, N, N), bf16),
            pltpu.VMEM((Z, C, T, N, N), bf16),
            pltpu.VMEM((Z, C, N, T * N), bf16),
            pltpu.VMEM((Z, C, 2, N, N), bf16),
            pltpu.VMEM((2, N, N), f32),
            pltpu.VMEM((2, 8, N), f32),
            pltpu.VMEM((2, 16, 8, N), f32),
            dma((5,)),
            dma((Y - 1,)), dma((Y - 1,)),
            dma((X,)), dma((Y,)),
            dma((Z, PIECES)), dma((Z, PIECES)),
            dma((Z, PIECES)), dma((Z, PIECES)),
            dma((Z, 2)), dma((Z, 3)),
            dma((Z,)), dma((Z,)),
            dma((2, 15)), dma((2, 15)),
        ],
        compiler_params=pltpu.CompilerParams(collective_id=0, has_side_effects=True, vmem_limit_bytes=24 << 20),
    )(live, block, dims, w, left, right)


def finish_kernel(tot_ref, rows_ref, cols_ref, w_ref, fg_ref, residual_ref, second_ref):
    tot = tot_ref[...]
    over = jnp.sum(tot[0:1], axis=1, keepdims=True)
    under = jnp.sum(tot[1:2], axis=1, keepdims=True)
    rayleigh = (over / under)[None]
    step = w_ref.shape[0]
    start = pl.multiple_of(pl.program_id(0) * step, step)
    first, image = [
        jnp.swapaxes(fg_ref[:, k, pl.ds(start, step)].astype(jnp.float32), 0, 1) for k in range(2)
    ]
    rows = rows_ref[pl.ds(start, step), :]
    state = w_ref[...].astype(jnp.float32) * cols_ref[...][None] * rows[:, None, :]
    residual_ref[...] = (first - rayleigh * state).astype(jnp.bfloat16)
    second_ref[...] = (image - rayleigh * first).astype(jnp.bfloat16)


def finish_call(tot, rows, cols, w, fg):
    step = 16
    sectors = w.shape[1]
    shape = jax.ShapeDtypeStruct(w.shape, w.dtype)
    slab = pl.BlockSpec((step, sectors, N), lambda i: (i, 0, 0))
    vmem = pl.BlockSpec(memory_space=pltpu.VMEM)
    return pl.pallas_call(
        finish_kernel,
        grid=(N // step,),
        out_shape=(shape, shape),
        in_specs=[vmem, vmem, vmem, slab, vmem],
        out_specs=(slab, slab),
        compiler_params=pltpu.CompilerParams(vmem_limit_bytes=24 << 20),
    )(tot, rows, cols, w, fg)


def body(wavefunction, left_env, right_env, term_live, block_live, sector_dims):
    arrays = (term_live.T, block_live, sector_dims, wavefunction, left_env, right_env)
    arrays = [pltpu.with_memory_space_constraint(array, pltpu.HBM) for array in arrays]
    fg, tot, rows, cols = images_call(*arrays)
    return finish_call(tot, rows, cols, wavefunction, fg.reshape(B, 2, N, N))


def solution(mesh):
    return jax.shard_map(
        body,
        mesh=mesh,
        in_specs=(
            P("sector", None, None),
            P("mpo", "sector", None),
            P("mpo", "sector", None),
            P("mpo", "sector"),
            P("sector", None),
            P(),
        ),
        out_specs=(P("sector", None, None), P("sector", None, None)),
        check_vma=False,
    )
```

```python
import jax
import jax.numpy as jnp
from jax import lax
from jax.experimental import pallas as pl
from jax.experimental.pallas import tpu as pltpu
from jax.sharding import PartitionSpec as P

MESH = pl.DeviceIdType.MESH
Y, Z, X, C = 4, 8, 4, 2
B = Z * X * C
N = 128
PAIR = 2
T = Y * PAIR
PIECES = 2


def wrap(value, size):
    return lax.rem(value + size, size)


def images_kernel(
    live_hbm, block_hbm, dims_hbm, w_ref, l_ref, r_ref,
    fg_ref, tot_ref, rows_ref, cols_ref,
    live_ref, block_ref, dims_ref, wide, wbuf, lown, lcat, rbuf, xbuf, own, sums, sent, got,
    in_sem, l_send, l_recv, r_send, r_recv, z_send, z_recv, c_send, c_recv,
    y_send, y_recv, f_send, o_sem, a_send, a_recv,
):
    y, s = lax.axis_index("mpo"), lax.axis_index("sector")
    z, x, c = s // (X * C), lax.rem(s // C, X), lax.rem(s, C)

    def place(y_at, z_at, x_at, c_at):
        return (y_at, (z_at * X + x_at) * C + c_at)

    def remote(src, dst, send, recv, device):
        return pltpu.make_async_remote_copy(
            src_ref=src, dst_ref=dst, send_sem=send, recv_sem=recv, device_id=device, device_id_type=MESH
        )

    here = place(y, z, x, c)
    z_near = [place(y, wrap(z + k, Z), x, c) for k in range(Z)]
    y_near = [place(wrap(y + k, Y), z, x, c) for k in range(Y)]
    sibling = place(y, z, x, 1 - c)
    plane = [place(wrap(y + i, Y), z, wrap(x + j, X), c) for i in range(Y) for j in range(X)][1:]
    line = [place(y, wrap(z + i, Z), x, wrap(c + j, C)) for i in range(Z) for j in range(C)][1:]

    barrier = pltpu.get_barrier_semaphore()
    for device in plane + line:
        pl.semaphore_signal(barrier, inc=1, device_id=device, device_id_type=MESH)
    sources = (live_hbm, l_ref, block_hbm, dims_hbm, w_ref)
    targets = (live_ref, lown, block_ref, dims_ref, wbuf)
    fetch = [pltpu.make_async_copy(src, dst, in_sem.at[k]) for k, (src, dst) in enumerate(zip(sources, targets))]
    for copy in fetch:
        copy.start()
    fetch[0].wait()
    fetch[1].wait()
    for k in range(PAIR):
        lown[k] = jnp.where(live_ref[0, k] > 0, lown[k].astype(jnp.float32), 0.0).astype(jnp.bfloat16)
    lcat[pl.ds(2 * y, PAIR)] = lown[...]
    pl.semaphore_wait(barrier, len(plane) + len(line))

    def row_copy(k):
        return remote(
            r_ref, rbuf.at[z, c, pl.ds(2 * y, PAIR)], r_send.at[k], r_recv.at[y], place(x, z, wrap(x + k, X), c)
        )

    for k in range(1, X):
        row_copy(k).start()

    @pl.when(x == y)
    def _():
        pltpu.make_async_copy(r_ref, rbuf.at[z, c, pl.ds(2 * y, PAIR)], r_recv.at[y]).start()

    @pl.when(x != y)
    def _():
        row_copy(0).start()

    def left_copy(k, device):
        from_y = wrap(y - k, Y) if device is here else y
        return remote(lown, lcat.at[pl.ds(2 * from_y, PAIR)], l_send.at[k - 1], l_recv.at[k - 1], device)

    for k in range(1, Y):
        left_copy(k, y_near[k]).start()

    for copy in fetch[2:]:
        copy.wait()

    def widen(i, carry):
        chunk = wbuf[pl.ds(i * 16, 16)].astype(jnp.float32)
        wide[pl.ds(i * 16 * B, 16 * B), :] = chunk.reshape(16 * B, N)
        return carry

    lax.fori_loop(0, N // 16, widen, 0)

    rows = lax.broadcasted_iota(jnp.int32, (N, N), 0)
    lanes = lax.broadcasted_iota(jnp.int32, (N, N), 1)
    own_dim = dims_ref[s]

    def used(b):
        return jnp.where(block_ref[0, b] > 0, dims_ref[b], 0)

    def masked(z_at, c_at):
        b = (z_at * X + y) * C + c_at
        mask = (rows < own_dim) & (lanes < used(b))
        return mask, jnp.where(mask, wide[pl.ds(b, N, stride=B), :], 0.0)

    def contract_left(vector):
        left = lcat[...].reshape(T * N, N)
        half = jnp.dot(left, vector, preferred_element_type=jnp.float32).astype(jnp.bfloat16)
        return half.reshape(T, N, half.shape[1])

    def beside(half):
        return jnp.concatenate([half[t] for t in range(T)], axis=1)

    def first_halves(z_at, carry):
        pair = [masked(z_at, c_at)[1].astype(jnp.bfloat16) for c_at in range(C)]
        half = contract_left(jnp.concatenate(pair, axis=1))
        for c_at in range(C):
            xbuf[z_at, c_at] = beside(half[:, :, c_at * N : (c_at + 1) * N])
        return carry

    sums[...] = jnp.zeros_like(sums)

    def images(z_at, c_at):
        mask, state = masked(z_at, c_at)
        right = rbuf[z_at, c_at].reshape(T * N, N)
        image = jnp.dot(xbuf[z_at, c_at], right, preferred_element_type=jnp.float32)
        first = jnp.where(mask, image, 0.0).astype(jnp.bfloat16)
        own[z_at, c_at, 0] = first
        image = jnp.dot(beside(contract_left(first)), right, preferred_element_type=jnp.float32)
        own[z_at, c_at, 1] = jnp.where(mask, image, 0.0).astype(jnp.bfloat16)

    def add_products(z_at):
        for c_at in range(C):
            state = masked(z_at, c_at)[1]
            sums[0] += state * own[z_at, c_at, 0].astype(jnp.float32)
            sums[1] += state * state

    order = [z]
    for d in range(1, Z // 2):
        order += [wrap(z - d, Z), wrap(z + d, Z)]
    order.append(wrap(z + Z // 2, Z))
    terms = T // PIECES

    def ring_copy(z_at, m, k, device):
        block = rbuf.at[z_at, c, pl.ds(k * terms, terms)]
        return remote(block, block, z_send.at[m, k], z_recv.at[m, k], device)

    def hand_over(m, k, c_at):
        block = rbuf.at[order[m], c_at, pl.ds(k * terms, terms)]
        return remote(block, block, c_send.at[m, k], c_recv.at[m, k], sibling)

    def onward(m):
        if m == 0:
            return [(order[0], 1, z_near[1]), (order[0], 2, z_near[Z - 1])]
        if m < Z - 3:
            return [(order[m], m + 2, z_near[1 if m % 2 else Z - 1])]
        if m == Z - 2:
            source = lax.select(c == 0, order[Z - 3], order[Z - 2])
            return [(source, Z - 1, place(y, lax.select(c == 0, wrap(z + 1, Z), wrap(z - 1, Z)), x, c))]
        return []

    def land(m, k):
        if m == 0:
            for p in range(k * terms // PAIR, (k + 1) * terms // PAIR):
                part = rbuf.at[z, c, pl.ds(PAIR * p, PAIR)]
                remote(part, part, r_send.at[0], r_recv.at[p], here).wait_recv()
        else:
            ring_copy(order[m], m, k, here).wait_recv()

    def pass_on(m, k):
        for z_at, to, device in onward(m):
            ring_copy(z_at, to, k, device).start()

    def ring(m, k):
        land(m, k)
        pass_on(m, k)
        hand_over(m, k, c).start()

    def keep_images(m):
        return pltpu.make_async_copy(own.at[order[m]], fg_ref.at[order[m], y], o_sem.at[m])

    def send_images(m, c_at, way):
        return remote(
            own.at[order[m], c_at], fg_ref.at[order[m], y, c_at],
            y_send.at[m, c_at, way], y_recv.at[m, c_at, way], y_near[(1, Y - 1)[way]],
        )

    def arrived(m, c_at, way):
        block = fg_ref.at[order[m], wrap(y + (3, 1, 2)[way], Y), c_at]
        return remote(block, block, y_send.at[m, c_at, 0], y_recv.at[m, c_at, way], here)

    def forward(m, c_at):
        way = (m + c_at) % 2
        block = fg_ref.at[order[m], wrap(y + (3, 1)[way], Y), c_at]
        return remote(block, block, f_send.at[m, c_at], y_recv.at[m, c_at, 2], y_near[(1, Y - 1)[way]])

    def pass_images(m):
        for c_at in range(C):
            arrived(m, c_at, (m + c_at) % 2).wait_recv()
            forward(m, c_at).start()

    def compute(m):
        for k in range(PIECES):
            hand_over(m, k, 1 - c).wait_recv()
        for c_at in range(C):
            images(order[m], c_at)
            for way in range(2):
                send_images(m, c_at, way).start()
        keep_images(m).start()
        add_products(order[m])

    def sum_copy(step, k):
        at = (z * C + c, y * X + x)[step]
        return remote(
            sent.at[step], got.at[step, at], a_send.at[step, k], a_recv.at[step, k], (line, plane)[step][k]
        )

    def start_sum(step):
        for k in range(15):
            sum_copy(step, k).start()
        got[step, (z * C + c, y * X + x)[step]] = sent[step]

    def end_sum(step):
        for k in range(15):
            sum_copy(step, k).wait()
        total = got[step, 0]
        for k in range(1, 16):
            total += got[step, k]
        return total

    ring(0, 0)
    land(0, 1)
    hand_over(0, 1, c).start()
    for k in range(1, Y):
        left_copy(k, here).wait_recv()
    first_halves(z, 0)
    pass_on(0, 1)
    compute(0)
    lax.fori_loop(1, Z, lambda k, carry: first_halves(wrap(z + k, Z), carry), 0)
    for d in range(1, Z // 2):
        near = (2 * d - 1, 2 * d)
        for m in near:
            ring(m, 0)
        if d == 3:
            pass_images(2)
        for m in near:
            ring(m, 1)
        for m in near:
            compute(m)
        pass_images((0, 1, 3)[d - 1])
    for k in range(PIECES):
        ring(Z - 1, k)
    compute(Z - 1)

    row = lax.broadcasted_iota(jnp.int32, (8, N), 0)
    part = [jnp.sum(sums[k], axis=0, keepdims=True) for k in range(2)]
    sent[0] = jnp.where(row == 0, part[0], 0.0) + jnp.where(row == 1, part[1], 0.0)
    start_sum(0)

    def columns(b, carry):
        cols_ref[pl.ds(b, 1), :] = jnp.where(lanes[:1] < used(b), 1.0, 0.0)
        return carry

    lax.fori_loop(0, B, columns, 0)
    rows_ref[...] = jnp.where(rows < own_dim, 1.0, 0.0)
    for m in range(Z - 4, Z - 2):
        pass_images(m)
    sent[1] = end_sum(0)
    start_sum(1)
    for m in range(Z - 2, Z):
        pass_images(m)
    tot_ref[...] = end_sum(1)

    for m in range(Z):
        keep_images(m).wait()
        for c_at in range(C):
            arrived(m, c_at, 1 - (m + c_at) % 2).wait_recv()
            arrived(m, c_at, 2).wait_recv()
            for way in range(2):
                send_images(m, c_at, way).wait_send()
            forward(m, c_at).wait_send()
        for k in range(PIECES):
            hand_over(m, k, c).wait_send()
            if m > 0:
                ring_copy(order[m], m, k, here).wait_send()
    for k in range(1, Y):
        left_copy(k, here).wait_send()
    for k in range(1, X):
        row_copy(k).wait_send()

    @pl.when(x != y)
    def _():
        row_copy(0).wait_send()


def images_call(live, block, dims, w, left, right):
    vmem = pl.BlockSpec(memory_space=pltpu.VMEM)
    dma = pltpu.SemaphoreType.DMA
    bf16, f32 = jnp.bfloat16, jnp.float32
    return pl.pallas_call(
        images_kernel,
        out_shape=(
            jax.ShapeDtypeStruct((Z, Y, C, 2, N, N), bf16),
            jax.ShapeDtypeStruct((8, N), f32),
            jax.ShapeDtypeStruct((N, N), f32),
            jax.ShapeDtypeStruct((B, N), f32),
        ),
        in_specs=[pl.BlockSpec(memory_space=pltpu.HBM)] * 6,
        out_specs=(pl.BlockSpec(memory_space=pl.ANY),) + (vmem,) * 3,
        scratch_shapes=[
            pltpu.SMEM((1, PAIR), jnp.int32),
            pltpu.SMEM((1, B), jnp.int32),
            pltpu.SMEM((B,), jnp.int32),
            pltpu.VMEM((N * B, N), f32),
            pltpu.VMEM((N, B, N), bf16),
            pltpu.VMEM((PAIR, N, N), bf16),
            pltpu.VMEM((T, N, N), bf16),
            pltpu.VMEM((Z, C, T, N, N), bf16),
            pltpu.VMEM((Z, C, N, T * N), bf16),
            pltpu.VMEM((Z, C, 2, N, N), bf16),
            pltpu.VMEM((2, N, N), f32),
            pltpu.VMEM((2, 8, N), f32),
            pltpu.VMEM((2, 16, 8, N), f32),
            dma((5,)),
            dma((Y - 1,)), dma((Y - 1,)),
            dma((X,)), dma((Y,)),
            dma((Z, PIECES)), dma((Z, PIECES)),
            dma((Z, PIECES)), dma((Z, PIECES)),
            dma((Z, C, 2)), dma((Z, C, 3)),
            dma((Z, C)), dma((Z,)),
            dma((2, 15)), dma((2, 15)),
        ],
        compiler_params=pltpu.CompilerParams(collective_id=0, has_side_effects=True, vmem_limit_bytes=24 << 20),
    )(live, block, dims, w, left, right)


def finish_kernel(tot_ref, rows_ref, cols_ref, w_ref, fg_ref, residual_ref, second_ref):
    tot = tot_ref[...]
    over = jnp.sum(tot[0:1], axis=1, keepdims=True)
    under = jnp.sum(tot[1:2], axis=1, keepdims=True)
    rayleigh = (over / under)[None]
    step = w_ref.shape[0]
    start = pl.multiple_of(pl.program_id(0) * step, step)
    first, image = [
        jnp.swapaxes(fg_ref[:, k, pl.ds(start, step)].astype(jnp.float32), 0, 1) for k in range(2)
    ]
    rows = rows_ref[pl.ds(start, step), :]
    state = w_ref[...].astype(jnp.float32) * cols_ref[...][None] * rows[:, None, :]
    residual_ref[...] = (first - rayleigh * state).astype(jnp.bfloat16)
    second_ref[...] = (image - rayleigh * first).astype(jnp.bfloat16)


def finish_call(tot, rows, cols, w, fg):
    step = 32
    sectors = w.shape[1]
    shape = jax.ShapeDtypeStruct(w.shape, w.dtype)
    slab = pl.BlockSpec((step, sectors, N), lambda i: (i, 0, 0))
    vmem = pl.BlockSpec(memory_space=pltpu.VMEM)
    return pl.pallas_call(
        finish_kernel,
        grid=(N // step,),
        out_shape=(shape, shape),
        in_specs=[vmem, vmem, vmem, slab, vmem],
        out_specs=(slab, slab),
        compiler_params=pltpu.CompilerParams(vmem_limit_bytes=24 << 20),
    )(tot, rows, cols, w, fg)


def body(wavefunction, left_env, right_env, term_live, block_live, sector_dims):
    arrays = (term_live.T, block_live, sector_dims, wavefunction, left_env, right_env)
    arrays = [pltpu.with_memory_space_constraint(array, pltpu.HBM) for array in arrays]
    fg, tot, rows, cols = images_call(*arrays)
    return finish_call(tot, rows, cols, wavefunction, fg.reshape(B, 2, N, N))


def solution(mesh):
    return jax.shard_map(
        body,
        mesh=mesh,
        in_specs=(
            P("sector", None, None),
            P("mpo", "sector", None),
            P("mpo", "sector", None),
            P("mpo", "sector"),
            P("sector", None),
            P(),
        ),
        out_specs=(P("sector", None, None), P("sector", None, None)),
        check_vma=False,
    )
```

```python
import jax
import jax.numpy as jnp
from jax import lax
from jax.experimental import pallas as pl
from jax.experimental.pallas import tpu as pltpu
from jax.sharding import PartitionSpec as P

MESH = pl.DeviceIdType.MESH
Y, Z, X, C = 4, 8, 4, 2
B = Z * X * C
N = 128
PAIR = 2
T = Y * PAIR
PIECES = 2


def wrap(value, size):
    return lax.rem(value + size, size)


def images_kernel(
    live_hbm, block_hbm, dims_hbm, w_ref, l_ref, r_ref,
    fg_ref, tot_ref, rows_ref, cols_ref,
    live_ref, block_ref, dims_ref, wide, wbuf, lown, lcat, rbuf, xbuf, own, sums, sent, got,
    in_sem, l_send, l_recv, r_send, r_recv, z_send, z_recv, c_send, c_recv,
    y_send, y_recv, f_send, o_sem, a_send, a_recv,
):
    y, s = lax.axis_index("mpo"), lax.axis_index("sector")
    z, x, c = s // (X * C), lax.rem(s // C, X), lax.rem(s, C)

    def place(y_at, z_at, x_at, c_at):
        return (y_at, (z_at * X + x_at) * C + c_at)

    def remote(src, dst, send, recv, device):
        return pltpu.make_async_remote_copy(
            src_ref=src, dst_ref=dst, send_sem=send, recv_sem=recv, device_id=device, device_id_type=MESH
        )

    here = place(y, z, x, c)
    z_near = [place(y, wrap(z + k, Z), x, c) for k in range(Z)]
    y_near = [place(wrap(y + k, Y), z, x, c) for k in range(Y)]
    sibling = place(y, z, x, 1 - c)
    plane = [place(wrap(y + i, Y), z, wrap(x + j, X), c) for i in range(Y) for j in range(X)][1:]
    line = [place(y, wrap(z + i, Z), x, wrap(c + j, C)) for i in range(Z) for j in range(C)][1:]

    barrier = pltpu.get_barrier_semaphore()
    for device in plane + line:
        pl.semaphore_signal(barrier, inc=1, device_id=device, device_id_type=MESH)
    sources = (live_hbm, l_ref, block_hbm, dims_hbm, w_ref)
    targets = (live_ref, lown, block_ref, dims_ref, wbuf)
    fetch = [pltpu.make_async_copy(src, dst, in_sem.at[k]) for k, (src, dst) in enumerate(zip(sources, targets))]
    for copy in fetch:
        copy.start()
    fetch[0].wait()
    fetch[1].wait()
    for k in range(PAIR):
        lown[k] = jnp.where(live_ref[0, k] > 0, lown[k].astype(jnp.float32), 0.0).astype(jnp.bfloat16)
    lcat[pl.ds(2 * y, PAIR)] = lown[...]
    pl.semaphore_wait(barrier, len(plane) + len(line))

    def row_copy(k):
        return remote(
            r_ref, rbuf.at[z, c, pl.ds(2 * y, PAIR)], r_send.at[k], r_recv.at[y], place(x, z, wrap(x + k, X), c)
        )

    for k in range(1, X):
        row_copy(k).start()

    @pl.when(x == y)
    def _():
        pltpu.make_async_copy(r_ref, rbuf.at[z, c, pl.ds(2 * y, PAIR)], r_recv.at[y]).start()

    @pl.when(x != y)
    def _():
        row_copy(0).start()

    def left_copy(k, device):
        from_y = wrap(y - k, Y) if device is here else y
        return remote(lown, lcat.at[pl.ds(2 * from_y, PAIR)], l_send.at[k - 1], l_recv.at[k - 1], device)

    for k in range(1, Y):
        left_copy(k, y_near[k]).start()

    for copy in fetch[2:]:
        copy.wait()

    def widen(i, carry):
        chunk = wbuf[pl.ds(i * 16, 16)].astype(jnp.float32)
        wide[pl.ds(i * 16 * B, 16 * B), :] = chunk.reshape(16 * B, N)
        return carry

    lax.fori_loop(0, N // 16, widen, 0)

    rows = lax.broadcasted_iota(jnp.int32, (N, N), 0)
    lanes = lax.broadcasted_iota(jnp.int32, (N, N), 1)
    own_dim = dims_ref[s]

    def used(b):
        return jnp.where(block_ref[0, b] > 0, dims_ref[b], 0)

    def masked(z_at, c_at):
        b = (z_at * X + y) * C + c_at
        mask = (rows < own_dim) & (lanes < used(b))
        return mask, jnp.where(mask, wide[pl.ds(b, N, stride=B), :], 0.0)

    def contract_left(vector):
        left = lcat[...].reshape(T * N, N)
        half = jnp.dot(left, vector, preferred_element_type=jnp.float32).astype(jnp.bfloat16)
        return half.reshape(T, N, half.shape[1])

    def beside(half):
        return jnp.concatenate([half[t] for t in range(T)], axis=1)

    def first_halves(z_at, carry):
        pair = [masked(z_at, c_at)[1].astype(jnp.bfloat16) for c_at in range(C)]
        half = contract_left(jnp.concatenate(pair, axis=1))
        for c_at in range(C):
            xbuf[z_at, c_at] = beside(half[:, :, c_at * N : (c_at + 1) * N])
        return carry

    sums[...] = jnp.zeros_like(sums)

    def images(z_at, c_at):
        mask, state = masked(z_at, c_at)
        right = rbuf[z_at, c_at].reshape(T * N, N)
        image = jnp.dot(xbuf[z_at, c_at], right, preferred_element_type=jnp.float32)
        first = jnp.where(mask, image, 0.0).astype(jnp.bfloat16)
        own[z_at, c_at, 0] = first
        image = jnp.dot(beside(contract_left(first)), right, preferred_element_type=jnp.float32)
        own[z_at, c_at, 1] = jnp.where(mask, image, 0.0).astype(jnp.bfloat16)

    def add_products(z_at):
        for c_at in range(C):
            state = masked(z_at, c_at)[1]
            sums[0] += state * own[z_at, c_at, 0].astype(jnp.float32)
            sums[1] += state * state

    order = [z]
    for d in range(1, Z // 2):
        order += [wrap(z - d, Z), wrap(z + d, Z)]
    order.append(wrap(z + Z // 2, Z))
    terms = T // PIECES

    def ring_copy(z_at, m, k, device):
        block = rbuf.at[z_at, c, pl.ds(k * terms, terms)]
        return remote(block, block, z_send.at[m, k], z_recv.at[m, k], device)

    def hand_over(m, k, c_at):
        block = rbuf.at[order[m], c_at, pl.ds(k * terms, terms)]
        return remote(block, block, c_send.at[m, k], c_recv.at[m, k], sibling)

    def onward(m):
        if m == 0:
            return [(order[0], 1, z_near[1]), (order[0], 2, z_near[Z - 1])]
        if m < Z - 3:
            return [(order[m], m + 2, z_near[1 if m % 2 else Z - 1])]
        if m == Z - 2:
            source = lax.select(c == 0, order[Z - 3], order[Z - 2])
            return [(source, Z - 1, place(y, lax.select(c == 0, wrap(z + 1, Z), wrap(z - 1, Z)), x, c))]
        return []

    def land(m, k):
        if m == 0:
            for p in range(k * terms // PAIR, (k + 1) * terms // PAIR):
                part = rbuf.at[z, c, pl.ds(PAIR * p, PAIR)]
                remote(part, part, r_send.at[0], r_recv.at[p], here).wait_recv()
        else:
            ring_copy(order[m], m, k, here).wait_recv()

    def pass_on(m, k):
        for z_at, to, device in onward(m):
            ring_copy(z_at, to, k, device).start()

    def ring(m, k):
        land(m, k)
        pass_on(m, k)
        hand_over(m, k, c).start()

    def keep_images(m):
        return pltpu.make_async_copy(own.at[order[m]], fg_ref.at[order[m], y], o_sem.at[m])

    def send_images(m, c_at, way):
        return remote(
            own.at[order[m], c_at], fg_ref.at[order[m], y, c_at],
            y_send.at[m, c_at, way], y_recv.at[m, c_at, way], y_near[(1, Y - 1)[way]],
        )

    def arrived(m, c_at, way):
        block = fg_ref.at[order[m], wrap(y + (3, 1, 2)[way], Y), c_at]
        return remote(block, block, y_send.at[m, c_at, 0], y_recv.at[m, c_at, way], here)

    def forward(m, c_at):
        way = (m + c_at) % 2
        block = fg_ref.at[order[m], wrap(y + (3, 1)[way], Y), c_at]
        return remote(block, block, f_send.at[m, c_at], y_recv.at[m, c_at, 2], y_near[(1, Y - 1)[way]])

    def pass_images(m):
        for c_at in range(C):
            arrived(m, c_at, (m + c_at) % 2).wait_recv()
            forward(m, c_at).start()

    def compute(m):
        for k in range(PIECES):
            hand_over(m, k, 1 - c).wait_recv()
        for c_at in range(C):
            images(order[m], c_at)
            for way in range(2):
                send_images(m, c_at, way).start()
        keep_images(m).start()
        add_products(order[m])

    def sum_copy(step, k):
        at = (z * C + c, y * X + x)[step]
        return remote(
            sent.at[step], got.at[step, at], a_send.at[step, k], a_recv.at[step, k], (line, plane)[step][k]
        )

    def start_sum(step):
        for k in range(15):
            sum_copy(step, k).start()
        got[step, (z * C + c, y * X + x)[step]] = sent[step]

    def end_sum(step):
        for k in range(15):
            sum_copy(step, k).wait()
        total = got[step, 0]
        for k in range(1, 16):
            total += got[step, k]
        return total

    ring(0, 0)
    land(0, 1)
    hand_over(0, 1, c).start()
    for k in range(1, Y):
        left_copy(k, here).wait_recv()
    first_halves(z, 0)
    pass_on(0, 1)
    compute(0)
    lax.fori_loop(1, Z, lambda k, carry: first_halves(wrap(z + k, Z), carry), 0)
    for d in range(1, Z // 2):
        near = (2 * d - 1, 2 * d)
        for m in near:
            ring(m, 0)
        if d == 3:
            pass_images(2)
        for m in near:
            ring(m, 1)
        for m in near:
            compute(m)
        if d < 3:
            pass_images(d - 1)
    for k in range(PIECES):
        ring(Z - 1, k)
    compute(Z - 1)

    row = lax.broadcasted_iota(jnp.int32, (8, N), 0)
    part = [jnp.sum(sums[k], axis=0, keepdims=True) for k in range(2)]
    sent[0] = jnp.where(row == 0, part[0], 0.0) + jnp.where(row == 1, part[1], 0.0)
    start_sum(0)

    def columns(b, carry):
        cols_ref[pl.ds(b, 1), :] = jnp.where(lanes[:1] < used(b), 1.0, 0.0)
        return carry

    lax.fori_loop(0, B, columns, 0)
    rows_ref[...] = jnp.where(rows < own_dim, 1.0, 0.0)
    for m in range(Z - 5, Z - 2):
        pass_images(m)
    sent[1] = end_sum(0)
    start_sum(1)
    for m in range(Z - 2, Z):
        pass_images(m)
    tot_ref[...] = end_sum(1)

    for m in range(Z):
        keep_images(m).wait()
        for c_at in range(C):
            arrived(m, c_at, 1 - (m + c_at) % 2).wait_recv()
            arrived(m, c_at, 2).wait_recv()
            for way in range(2):
                send_images(m, c_at, way).wait_send()
            forward(m, c_at).wait_send()
        for k in range(PIECES):
            hand_over(m, k, c).wait_send()
            if m > 0:
                ring_copy(order[m], m, k, here).wait_send()
    for k in range(1, Y):
        left_copy(k, here).wait_send()
    for k in range(1, X):
        row_copy(k).wait_send()

    @pl.when(x != y)
    def _():
        row_copy(0).wait_send()


def images_call(live, block, dims, w, left, right):
    vmem = pl.BlockSpec(memory_space=pltpu.VMEM)
    dma = pltpu.SemaphoreType.DMA
    bf16, f32 = jnp.bfloat16, jnp.float32
    return pl.pallas_call(
        images_kernel,
        out_shape=(
            jax.ShapeDtypeStruct((Z, Y, C, 2, N, N), bf16),
            jax.ShapeDtypeStruct((8, N), f32),
            jax.ShapeDtypeStruct((N, N), f32),
            jax.ShapeDtypeStruct((B, N), f32),
        ),
        in_specs=[pl.BlockSpec(memory_space=pltpu.HBM)] * 6,
        out_specs=(pl.BlockSpec(memory_space=pl.ANY),) + (vmem,) * 3,
        scratch_shapes=[
            pltpu.SMEM((1, PAIR), jnp.int32),
            pltpu.SMEM((1, B), jnp.int32),
            pltpu.SMEM((B,), jnp.int32),
            pltpu.VMEM((N * B, N), f32),
            pltpu.VMEM((N, B, N), bf16),
            pltpu.VMEM((PAIR, N, N), bf16),
            pltpu.VMEM((T, N, N), bf16),
            pltpu.VMEM((Z, C, T, N, N), bf16),
            pltpu.VMEM((Z, C, N, T * N), bf16),
            pltpu.VMEM((Z, C, 2, N, N), bf16),
            pltpu.VMEM((2, N, N), f32),
            pltpu.VMEM((2, 8, N), f32),
            pltpu.VMEM((2, 16, 8, N), f32),
            dma((5,)),
            dma((Y - 1,)), dma((Y - 1,)),
            dma((X,)), dma((Y,)),
            dma((Z, PIECES)), dma((Z, PIECES)),
            dma((Z, PIECES)), dma((Z, PIECES)),
            dma((Z, C, 2)), dma((Z, C, 3)),
            dma((Z, C)), dma((Z,)),
            dma((2, 15)), dma((2, 15)),
        ],
        compiler_params=pltpu.CompilerParams(collective_id=0, has_side_effects=True, vmem_limit_bytes=24 << 20),
    )(live, block, dims, w, left, right)


def finish_kernel(tot_ref, rows_ref, cols_ref, w_ref, fg_ref, residual_ref, second_ref):
    tot = tot_ref[...]
    over = jnp.sum(tot[0:1], axis=1, keepdims=True)
    under = jnp.sum(tot[1:2], axis=1, keepdims=True)
    rayleigh = (over / under)[None]
    step = w_ref.shape[0]
    start = pl.multiple_of(pl.program_id(0) * step, step)
    first, image = [
        jnp.swapaxes(fg_ref[:, k, pl.ds(start, step)].astype(jnp.float32), 0, 1) for k in range(2)
    ]
    rows = rows_ref[pl.ds(start, step), :]
    state = w_ref[...].astype(jnp.float32) * cols_ref[...][None] * rows[:, None, :]
    residual_ref[...] = (first - rayleigh * state).astype(jnp.bfloat16)
    second_ref[...] = (image - rayleigh * first).astype(jnp.bfloat16)


def finish_call(tot, rows, cols, w, fg):
    step = 32
    sectors = w.shape[1]
    shape = jax.ShapeDtypeStruct(w.shape, w.dtype)
    slab = pl.BlockSpec((step, sectors, N), lambda i: (i, 0, 0))
    vmem = pl.BlockSpec(memory_space=pltpu.VMEM)
    return pl.pallas_call(
        finish_kernel,
        grid=(N // step,),
        out_shape=(shape, shape),
        in_specs=[vmem, vmem, vmem, slab, vmem],
        out_specs=(slab, slab),
        compiler_params=pltpu.CompilerParams(vmem_limit_bytes=24 << 20),
    )(tot, rows, cols, w, fg)


def body(wavefunction, left_env, right_env, term_live, block_live, sector_dims):
    arrays = (term_live.T, block_live, sector_dims, wavefunction, left_env, right_env)
    arrays = [pltpu.with_memory_space_constraint(array, pltpu.HBM) for array in arrays]
    fg, tot, rows, cols = images_call(*arrays)
    return finish_call(tot, rows, cols, wavefunction, fg.reshape(B, 2, N, N))


def solution(mesh):
    return jax.shard_map(
        body,
        mesh=mesh,
        in_specs=(
            P("sector", None, None),
            P("mpo", "sector", None),
            P("mpo", "sector", None),
            P("mpo", "sector"),
            P("sector", None),
            P(),
        ),
        out_specs=(P("sector", None, None), P("sector", None, None)),
        check_vma=False,
    )
```
